32 devices in a mesh: groups: 2 (over y), row: 4 (over x, core), col: 4 (over z).
Axes of the slice: x: 2, y: 2, z: 4, core: 2. Of those that a mesh axis runs over, the one named last changes fastest.
Arguments:
- features: float32 [16384, 256], P(('groups', 'row', 'col')), parts along dimension 0, may hold values from -6 to 6
- weight: float32 [256, 256], replicated, may hold values from -0.375 to 0.375
- cotangent: float32 [16384, 256], P(('groups', 'row', 'col')), parts along dimension 0, may hold values from -6 to 6
- column_of: int32 [16384, 1], P(('groups', 'row', 'col')), parts along dimension 0, may hold values from 0 to 3; in each aligned block of 512 rows (0 to 511, 512 to 1023, ...) at most 256 rows name the same one
- block_rows: int32 [32, 32], P(('groups', 'row', 'col')), parts along dimension 0, may hold values from 0 to 15
- block_cols: int32 [32, 32], P(('groups', 'row', 'col')), parts along dimension 0, may hold values from 0 to 7
- edge_blocks: float32 [32, 32, 128, 128], P(('groups', 'row', 'col')), parts along dimension 0, may hold values from -0.25 to 0.25
Outputs:
- activated: float32 [16384, 256], P(('groups', 'row', 'col')), parts along dimension 0
- input_grad: float32 [16384, 256], P(('groups', 'row', 'col')), parts along dimension 0
- weight_grad: float32 [512, 256], P('groups'), parts along dimension 0
The draws below stay inside these ranges and needn't reach their ends.
There are 2 independent parts, one for each index of `groups`. The reference program is written for one: setup_inputs(seed, part) draws one part's arguments, and reference() takes and returns one part's arrays. A program takes and returns all parts, laid end to end along the dimension named above; an argument that names none is the same for every part. Nothing has to cross between parts.
Inputs may be any that keep to these rules, and one draw needn't show every extreme that they name: `column_of`: among the 512 rows of one device no grid column is named by more than 256 rows, and on some devices some grid column by exactly 256. `block_rows`: A pair of destination and source block may be listed more than once in a tile; the listed blocks then add.
All inputs are finite; a program needn't handle non-finite values.
Results may differ from the reference program's by a relative error of at most 0.0003.
Values sent between devices are 32-bit elements; how exact they have to be, the bound alone decides.
A program may use at most 64 MiB of HBM per device.

```python
import math
import jax
import jax.numpy as jnp
import numpy as np
from jax import lax

F = 256
BLOCK = 128
RD = 512
NODES = 8192
CAP = 256
DB = 16
SB = 8
KT = 32
TILES = 16
N_ROW = 4
N_COL = 4


def touch_ends(array, stream_key, least, top_value):
    longest = array.shape.index(max(array.shape))
    spots = []
    for shift in (0, 1):
        where = [jax.random.randint(jax.random.fold_in(stream_key, axis), (), 0, length) for axis, length in enumerate(array.shape)]
        where[longest] = (where[longest] + shift) % array.shape[longest]
        spots.append(tuple(where))
    return array.at[spots[0]].set(least).at[spots[1]].set(top_value)


def block_scale(key, shape, pieces, smallest, top_value):
    loudness, own = 1.0, jax.random.fold_in(key, 6)
    for axis_at, shards_of in pieces:
        heights = jnp.exp(jax.random.uniform(jax.random.fold_in(own, axis_at), (shards_of,), jnp.float32, smallest / len(pieces), top_value / len(pieces)))
        loudness = loudness * jnp.repeat(heights, shape[axis_at] // shards_of).reshape([-1 if axis == axis_at else 1 for axis in range(len(shape))])
    return loudness


def shared_out(rng, own, number, rows, amount, top, reach, slope):
    ranking = jax.random.permutation(rng, amount)
    packed, usual = load_shares(amount, rows * top, reach, slope, True), load_shares(amount, rows * top, reach, slope, False)
    places = jnp.arange(amount)

    def named(sizes, turn):
        used = int((sizes > 0).sum())
        fixed = max(1, used // 4)
        passed = fixed + (places - fixed + turn * (used - fixed)) % max(1, amount - fixed)
        return jnp.zeros((amount,), jnp.int32).at[ranking[jnp.where(places < fixed, places, passed)]].set(jnp.asarray(sizes, jnp.int32))

    sizes = jnp.where(number % 4 == 0, named(packed, number // 4), named(usual, number - number // 4 - 1))
    mixed = jax.random.permutation(jax.random.fold_in(own, 3), amount)
    source_of, sink = mixed[0:amount // 2 * 2:2], mixed[1:amount // 2 * 2:2]
    margin = jnp.minimum(sizes[source_of] - 1, reach - sizes[sink]) // 2
    margin = jnp.where((source_of == ranking[0]) | (sink == ranking[0]) | (sizes[sink] == 0), 0, jnp.maximum(margin, 0))
    passed = jax.random.randint(jax.random.fold_in(own, 4), (amount // 2,), 0, 1 << 20) % (margin + 1)
    sizes = sizes.at[source_of].add(-passed).at[sink].add(passed)
    labels = jnp.searchsorted(jnp.cumsum(sizes), jnp.arange(rows * top), side="right").astype(jnp.int32)
    grid = labels.reshape(top, rows).T
    grid = grid[jax.random.permutation(jax.random.fold_in(own, 1), rows)]
    turn = jax.random.randint(jax.random.fold_in(own, 2), (rows, 1), 0, top)
    return jnp.take_along_axis(grid, (jnp.arange(top)[None, :] + turn) % top, axis=1)


def load_shares(amount, total, most, slope, full):
    weights = [(1 << 20) // math.isqrt(grade ** slope) + 1 for grade in range(1, amount + 1)]
    largest = most if full else min(most, max(-(-total // amount), total * weights[0] // sum(weights)))
    least = 1 if total - largest >= amount - 1 else 0
    holding, rest = [largest] + [least] * (amount - 1), total - largest - least * (amount - 1)
    while rest > 0:
        candidates = [i for i in range(1, amount) if holding[i] < largest] or [i for i in range(1, amount) if holding[i] < most]
        pool, remaining = sum([weights[i] for i in candidates]), rest
        for i in candidates:
            extra = min(most - holding[i], max(1, remaining * weights[i] // pool), rest)
            holding[i] = holding[i] + extra
            rest = rest - extra
    return np.array(holding)


def bell_draw(rng, shape, scale, reach, split=(), kind=jnp.bfloat16):
    drawn = scale * jax.random.normal(rng, shape, jnp.float32)
    if split:
        drawn = drawn * block_scale(rng, shape, split, -0.22, 0.18)
    return jnp.clip(drawn, -reach, reach).astype(kind)


def setup_inputs(seed: int = 0, part: int = 0) -> dict:
    splits = jax.random.split(jax.random.key(seed), 8)
    part_splits = jax.random.split(jax.random.fold_in(splits[7], part), 8)
    features = bell_draw(part_splits[0], (NODES, F), 1.0, 6.0, ((0, 16),), jnp.float32)
    weight = bell_draw(splits[1], (F, F), F ** -0.5, 0.375, (), jnp.float32)
    cotangent = bell_draw(part_splits[2], (NODES, F), 1.0, 6.0, ((0, 16),), jnp.float32)
    column_of_keys = jax.random.split(jax.random.fold_in(part_splits[3], 1), NODES // RD)
    column_of_turns = jax.random.permutation(jax.random.fold_in(part_splits[3], 3), NODES // RD)
    column_of = jax.vmap(lambda own, number: shared_out(jax.random.fold_in(part_splits[3], 2), own, number, RD, N_COL, 1, CAP, 2))(column_of_keys, column_of_turns).reshape((NODES, 1))
    block_rows = touch_ends(jax.random.randint(part_splits[4], (TILES, KT), 0, DB), jax.random.fold_in(part_splits[4], 1), 0, DB - 1).astype(jnp.int32)
    block_cols = touch_ends(jax.random.randint(part_splits[5], (TILES, KT), 0, SB), jax.random.fold_in(part_splits[5], 1), 0, SB - 1).astype(jnp.int32)
    edge_blocks = bell_draw(part_splits[6], (TILES, KT, BLOCK, BLOCK), (N_ROW * BLOCK) ** -0.5, 0.25, ((0, 16),), jnp.float32)
    return {"features": features, "weight": weight, "cotangent": cotangent, "column_of": column_of, "block_rows": block_rows, "block_cols": block_cols, "edge_blocks": edge_blocks}


precise = lax.Precision.HIGHEST

def activate(value):
    return jax.nn.gelu(value, approximate=True)

def slot_positions(column_of):
    target = column_of[:, 0].reshape(N_ROW * N_COL, RD)
    onehot = (target[:, :, None] == jnp.arange(N_COL, dtype=jnp.int32)[None, None, :]).astype(jnp.int32)
    earlier = jnp.cumsum(onehot, axis=1) - onehot
    slot_rank = lax.optimization_barrier(jnp.sum(earlier * onehot, axis=2))
    owner = jnp.arange(N_ROW * N_COL, dtype=jnp.int32)[:, None]
    tile_index = (owner // N_COL * N_COL + target).reshape(-1)
    slot_index = (owner % N_COL * CAP + slot_rank).reshape(-1)
    return (tile_index, slot_index)

def reference(features, weight, cotangent, column_of, block_rows, block_cols, edge_blocks):
    tile_index, slot_index = slot_positions(column_of)
    transformed = jnp.dot(features, weight, precision=precise, preferred_element_type=jnp.float32)
    sources = jnp.zeros((N_ROW * N_COL, N_COL * CAP, F), jnp.float32).at[tile_index, slot_index].set(transformed)

    def column_sum(column):

        def one_tile(total, grid_row):
            tile = grid_row * N_COL + column
            slots = sources[tile].reshape(SB, BLOCK, F)
            picked = slots[block_cols[tile]]
            products = jnp.einsum('kij,kjf->kif', edge_blocks[tile], picked, precision=precise)
            return (total.at[block_rows[tile]].add(products), None)
        total, _ = lax.scan(one_tile, jnp.zeros((DB, BLOCK, F), jnp.float32), jnp.arange(N_ROW, dtype=jnp.int32))
        return total.reshape(N_ROW, RD, F)
    aggregated = lax.map(column_sum, jnp.arange(N_COL, dtype=jnp.int32))
    aggregated = jnp.transpose(aggregated, (1, 0, 2, 3)).reshape(NODES, F)
    activated, pullback = jax.vjp(activate, aggregated)
    grad_pre, = pullback(cotangent)
    by_column = jnp.transpose(grad_pre.reshape(N_ROW, N_COL, RD, F), (1, 0, 2, 3)).reshape(N_COL, DB, BLOCK, F)

    def tile_grad(tile):
        column = tile % N_COL
        picked = by_column[column][block_rows[tile]]
        products = jnp.einsum('kji,kjf->kif', edge_blocks[tile], picked, precision=precise)
        return jnp.zeros((SB, BLOCK, F), jnp.float32).at[block_cols[tile]].add(products).reshape(N_COL * CAP, F)
    slot_grad = lax.map(tile_grad, jnp.arange(N_ROW * N_COL, dtype=jnp.int32))
    node_grad = slot_grad[tile_index, slot_index]
    input_grad = jnp.dot(node_grad, weight.T, precision=precise, preferred_element_type=jnp.float32)
    weight_grad = jnp.dot(features.T, node_grad, precision=precise, preferred_element_type=jnp.float32)
    weight_grad = weight_grad * float(NODES) ** (-0.5)
    return (activated, input_grad, weight_grad)
```

```python
import functools
import math

import jax
import jax.numpy as jnp
from jax import lax
from jax.experimental import pallas as pl
from jax.experimental.pallas import tpu as pltpu
from jax.sharding import PartitionSpec as P

MESH = pl.DeviceIdType.MESH
F32, BF16, I32 = jnp.float32, jnp.bfloat16, jnp.int32
PARTS = 2


def split(value):
    high = value.astype(BF16)
    return high, (value - high.astype(F32)).astype(BF16)


def wide(value):
    return jnp.concatenate(split(value), axis=1)


def mm(a, b, dims=((1,), (0,))):
    return lax.dot_general(a, b, (dims, ((), ())), preferred_element_type=F32)


def mm3(a, b, dims=((1,), (0,))):
    return mm(a[0], b[0], dims) + mm(a[1], b[0], dims) + mm(a[0], b[1], dims)


def each(start, stop, body):
    if stop - start <= 8:
        for i in range(start, stop):
            body(i)
    else:

        def step(i, carry):
            body(i)
            return carry

        lax.fori_loop(start, stop, step, 0)


def order_of(own, other, meta, base):
    count = own.shape[1]
    row_at = lax.broadcasted_iota(I32, (count, count), 0)
    lane_at = lax.broadcasted_iota(I32, (count, count), 1)

    def upright(v):
        return jnp.sum(jnp.where(row_at == lane_at, jnp.broadcast_to(v, row_at.shape), 0), axis=1, keepdims=True)

    own_up, other_up = upright(own), upright(other)
    before = (own < own_up) | ((own == own_up) & (lane_at < row_at))
    rank = jnp.sum(before.astype(I32), axis=1, keepdims=True)
    placed = rank == lane_at

    def lay(v):
        return jnp.sum(jnp.where(placed, v, 0), axis=0, keepdims=True)

    meta[base : base + 1, :count] = lay(row_at)
    meta[base + 1 : base + 2, :count] = lay(jnp.broadcast_to(own_up, row_at.shape))
    meta[base + 2 : base + 3, :count] = lay(jnp.broadcast_to(other_up, row_at.shape))
    meta[base + 3 : base + 4, :count] = jnp.maximum(
        jnp.sum((own_up <= lane_at).astype(I32), axis=0, keepdims=True) - 1, 0
    )
    meta[base + 4 : base + 5, :count] = jnp.sum((own_up == lane_at).astype(I32), axis=0, keepdims=True)


def kernel(
    sizes,
    features_hbm, weight_ref, cotangent_hbm, column_ref, rows_ref, cols_ref, edges_hbm,
    activated_ref, input_ref, wgrad_ref,
    feat, cot, edges, edge_f, edge_b, meta, plan, onehot, onehot_t,
    send, recv, table, run, dest, near, mid, far, agg, every, back, back_in,
    wpart, wrow, wsum, wcol, wown, wall,
    load_sem, a_send, a_recv, n_send, n_recv, g_send, g_recv, b_send, b_recv,
    wr_send, wr_recv, wz_send, wz_recv, wy_send, wy_recv, wx_send, wx_recv,
):
    n_row, n_col, cap, block, d_blocks, s_blocks, reducers = sizes
    count = edges.shape[0]
    rd, width = feat.shape
    half = width // PARTS
    row, col = lax.axis_index("row"), lax.axis_index("col")
    p1 = row + 1 - 2 * lax.rem(row, 2)
    p2 = lax.rem(row + 2, n_row)
    p3 = lax.rem(p1 + 2, n_row)

    def remote(src, dst, s_sem, r_sem, where):
        return pltpu.make_async_remote_copy(
            src_ref=src, dst_ref=dst, send_sem=s_sem, recv_sem=r_sem, device_id=where, device_id_type=MESH
        )

    barrier = pltpu.get_barrier_semaphore()
    each(1, n_row, lambda k: pl.semaphore_signal(
        barrier, inc=1, device_id={"row": lax.rem(row + k, n_row)}, device_id_type=MESH))
    each(1, n_col, lambda k: pl.semaphore_signal(
        barrier, inc=1, device_id={"col": lax.rem(col + k, n_col)}, device_id_type=MESH))

    load_f = pltpu.make_async_copy(features_hbm, feat, load_sem.at[0])
    load_e = pltpu.make_async_copy(edges_hbm, edges, load_sem.at[1])
    load_c = pltpu.make_async_copy(cotangent_hbm, cot, load_sem.at[2])
    load_f.start()
    load_e.start()
    load_c.start()

    target = column_ref[...]
    named = lax.broadcasted_iota(I32, (rd, 128), 1) == target
    below = lax.broadcasted_iota(I32, (rd, rd), 1) < lax.broadcasted_iota(I32, (rd, rd), 0)
    earlier = mm(below.astype(F32).astype(BF16), named.astype(F32).astype(BF16))
    rank = jnp.sum(jnp.where(named, earlier, 0.0), axis=1, keepdims=True)
    slot = target * cap + rank.astype(I32)
    same = lax.broadcasted_iota(I32, (rd, rd), 1) == lax.broadcasted_iota(I32, (rd, rd), 0)
    slot_row = jnp.sum(jnp.where(same, jnp.broadcast_to(slot, (rd, rd)), 0), axis=0, keepdims=True)
    slots = n_col * cap
    onehot[...] = (lax.broadcasted_iota(I32, (slots, rd), 0) == slot_row).astype(F32).astype(BF16)
    load_f.wait()

    def route_copy(part, k):
        to = lax.rem(col + k, n_col)
        return remote(
            send.at[part, pl.ds(pl.multiple_of(to * cap, cap), cap)],
            recv.at[part, pl.ds(pl.multiple_of(col * cap, cap), cap)],
            a_send.at[part, to], a_recv.at[part, col], {"col": to},
        )

    def route_arrival(part, k):
        of = lax.rem(col + k, n_col)
        return remote(
            send.at[part, pl.ds(pl.multiple_of(of * cap, cap), cap)],
            recv.at[part, pl.ds(pl.multiple_of(of * cap, cap), cap)],
            a_send.at[part, of], a_recv.at[part, of], {"col": of},
        )

    mine = pl.ds(pl.multiple_of(col * cap, cap), cap)
    for part in range(PARTS):
        both = mm(onehot[...], wide(feat[:, part * half : (part + 1) * half]))
        send[part] = both[:, :half] + both[:, half:]
        if part == 0:
            pl.semaphore_wait(barrier, n_row + n_col - 2)
        each(1, n_col, lambda k: route_copy(part, k).start())
        recv[part, mine] = send[part, mine]

    order_of(rows_ref[...], cols_ref[...], meta, 0)
    order_of(cols_ref[...], rows_ref[...], meta, 8)
    load_m = pltpu.make_async_copy(meta, plan, load_sem.at[3])
    load_m.start()
    onehot_t[...] = (lax.broadcasted_iota(I32, (rd, slots), 1) == slot).astype(F32).astype(BF16)
    load_e.wait()

    def prepare(k, carry):
        value = edges[k]
        edge_f[k] = wide(value)
        edge_b[k] = wide(value.T)
        return carry

    lax.fori_loop(0, count, prepare, 0)
    load_m.wait()
    load_c.wait()
    w_pair = split(weight_ref[...])

    def fill(at, value):
        pair = wide(value)
        table[at, :block] = pair
        table[at, block:] = pair

    def multiply(edge_ref, base):
        def step(p, total):
            product = mm(edge_ref[plan[base, p]], table[plan[base + 2, p]])
            kept = plan[base + 1, p] == plan[base + 1, jnp.maximum(p - 1, 0)]
            total = jnp.where(kept, total, 0.0) + product[:, :half] + product[:, half:]
            run[p] = total
            return total

        lax.fori_loop(0, count, step, jnp.zeros((block, half), F32), unroll=8)

    def taken(base, at):
        return jnp.where(plan[base + 4, at] > 0, run[plan[base + 3, at]], 0.0)

    per = rd // block

    def near_copy(part, which):
        return remote(
            dest.at[part, p3 if which == 0 else p1], near.at[part, which],
            n_send.at[part, which], n_recv.at[part, which], {"row": p1},
        )

    def far_copy(part):
        return remote(mid.at[part], far.at[part], n_send.at[part, 2], n_recv.at[part, 2], {"row": p2})

    for part in range(PARTS):
        each(1, n_col, lambda k: route_arrival(part, k).wait_recv())
        for s in range(s_blocks):
            fill(s, recv[part, s * block : (s + 1) * block])
        multiply(edge_f, 0)
        for which, owner in enumerate((p3, p1, p2, row)):
            for i in range(per):
                dest[part, owner, i * block : (i + 1) * block] = taken(0, owner * per + i)
            if which < 2:
                near_copy(part, which).start()
        near_copy(part, 0).wait_recv()
        mid[part] = dest[part, p2] + near[part, 0]
        far_copy(part).start()

    for part in range(PARTS):
        near_copy(part, 1).wait_recv()
        far_copy(part).wait_recv()
        agg[:, part * half : (part + 1) * half] = dest[part, row] + near[part, 1] + far[part]

    agg_pair = split(agg[...])
    x = mm3(agg_pair, w_pair)
    scale = math.sqrt(2.0 / math.pi)
    square = x * x
    t = jnp.tanh(scale * (x + 0.044715 * (square * x)))
    activated_ref[...] = 0.5 * x * (1.0 + t)
    slope = 0.5 * (1.0 + t) + 0.5 * x * (1.0 - t * t) * (scale * (1.0 + 3.0 * 0.044715 * square))
    grad_pair = split(cot[...] * slope)
    grad = mm3(grad_pair, w_pair, ((1,), (1,)))

    def give(part, which):
        at = row if which < 2 else p2
        return remote(
            every.at[part, at], every.at[part, at],
            g_send.at[part, which], g_recv.at[part, which], {"row": p2 if which == 0 else p1},
        )

    def take(part, which):
        at = (p2, p1, p3)[which]
        return remote(
            every.at[part, at], every.at[part, at],
            g_send.at[part, which], g_recv.at[part, which], {"row": p2 if which == 0 else p1},
        )

    piece = width // n_row

    def w_row_copy(k):
        to = lax.rem(row + k, n_row)
        return remote(wpart.at[to], wrow.at[row], wr_send.at[to], wr_recv.at[row], {"row": to})

    def w_row_arrival(k):
        of = lax.rem(row + k, n_row)
        return remote(wpart.at[of], wrow.at[of], wr_send.at[of], wr_recv.at[of], {"row": of})

    for part in range(PARTS):
        every[part, row] = grad[:, part * half : (part + 1) * half]
        give(part, 0).start()
        give(part, 1).start()
        if part == 0:
            wlocal = mm3(agg_pair, grad_pair, ((0,), (0,)))
            for r in range(n_row):
                wpart[r] = wlocal[r * piece : (r + 1) * piece]
            each(1, n_row, lambda k: w_row_copy(k).start())

    def back_copy(part, k):
        to = lax.rem(col + k, n_col)
        return remote(
            back.at[part, pl.ds(pl.multiple_of(to * cap, cap), cap)],
            back_in.at[part, pl.ds(pl.multiple_of(col * cap, cap), cap)],
            b_send.at[part, to], b_recv.at[part, col], {"col": to},
        )

    def back_arrival(part, k):
        of = lax.rem(col + k, n_col)
        return remote(
            back.at[part, pl.ds(pl.multiple_of(of * cap, cap), cap)],
            back_in.at[part, pl.ds(pl.multiple_of(of * cap, cap), cap)],
            b_send.at[part, of], b_recv.at[part, of], {"col": of},
        )

    share = piece // reducers

    def w_col_copy(to):
        return remote(wsum.at[to], wcol.at[col], wz_send.at[to], wz_recv.at[col], {"col": to})

    def w_col_arrival(of):
        return remote(wsum.at[0], wcol.at[of], wz_send.at[0], wz_recv.at[of], {"col": of})

    def w_col_give(k):
        to = lax.rem(col + k, n_col)
        return remote(wown, wall.at[row, col], wy_send.at[to], wy_recv.at[col], {"col": to})

    def w_col_take(of):
        return remote(wown, wall.at[row, of], wy_send.at[of], wy_recv.at[of], {"col": of})

    def w_row_give(k):
        to = lax.rem(row + k, n_row)
        return remote(wall.at[row], wall.at[row], wx_send.at[to], wx_recv.at[row], {"row": to})

    def w_row_take(k):
        of = lax.rem(row + k, n_row)
        return remote(wall.at[of], wall.at[of], wx_send.at[of], wx_recv.at[of], {"row": of})

    def reducer(body):
        if reducers == n_col:
            body()
        else:
            pl.when(col < reducers)(body)

    def others(of, body):
        pl.when(of != col)(body)

    def w_second():
        each(1, n_row, lambda k: w_row_arrival(k).wait_recv())
        total = wpart[row]
        for k in range(1, n_row):
            total = total + wrow[lax.rem(row + k, n_row)]
        for j in range(reducers):
            wsum[j] = total[j * share : (j + 1) * share]
        if reducers == n_col:
            each(1, n_col, lambda k: w_col_copy(lax.rem(col + k, n_col)).start())
        else:
            each(0, reducers, lambda j: others(j, lambda: w_col_copy(j).start()))

    def w_third():
        def body():
            each(1, n_col, lambda k: w_col_arrival(lax.rem(col + k, n_col)).wait_recv())
            wcol[col] = wsum[col]
            total = wcol[0]
            for j in range(1, n_col):
                total = total + wcol[j]
            wown[...] = total * (float(rd * n_row * n_col) ** -0.5)
            each(1, n_col, lambda k: w_col_give(k).start())
            wall[row, col] = wown[...]

        reducer(body)

    def w_fourth():
        if reducers == n_col:
            each(1, n_col, lambda k: w_col_take(lax.rem(col + k, n_col)).wait_recv())
        else:
            each(0, reducers, lambda j: others(j, lambda: w_col_take(j).wait_recv()))
        each(1, n_row, lambda k: w_row_give(k).start())

    for part in range(PARTS):
        take(part, 0).wait_recv()
        give(part, 2).start()
        take(part, 1).wait_recv()
        take(part, 2).wait_recv()
        for owner in range(n_row):
            for i in range(per):
                fill(owner * per + i, every[part, owner, i * block : (i + 1) * block])
        multiply(edge_b, 8)
        for s in range(s_blocks):
            back[part, s * block : (s + 1) * block] = taken(8, s)
        each(1, n_col, lambda k: back_copy(part, k).start())
        back_in[part, mine] = back[part, mine]
        if part == 0:
            w_second()
        else:
            w_third()

    for part in range(PARTS):
        each(1, n_col, lambda k: back_arrival(part, k).wait_recv())
        both = mm(onehot_t[...], wide(back_in[part]))
        input_ref[:, part * half : (part + 1) * half] = both[:, :half] + both[:, half:]
        if part == 0:
            w_fourth()
    each(1, n_row, lambda k: w_row_take(k).wait_recv())
    for r in range(n_row):
        for j in range(reducers):
            wgrad_ref[r * piece + j * share : r * piece + (j + 1) * share] = wall[r, j]

    for part in range(PARTS):
        each(1, n_col, lambda k: route_copy(part, k).wait_send())
        each(1, n_col, lambda k: back_copy(part, k).wait_send())
        near_copy(part, 0).wait_send()
        near_copy(part, 1).wait_send()
        far_copy(part).wait_send()
        for which in range(3):
            give(part, which).wait_send()
    each(1, n_row, lambda k: w_row_copy(k).wait_send())
    each(1, n_row, lambda k: w_row_give(k).wait_send())
    if reducers == n_col:
        each(1, n_col, lambda k: w_col_copy(lax.rem(col + k, n_col)).wait_send())
    else:
        each(0, reducers, lambda j: others(j, lambda: w_col_copy(j).wait_send()))
    reducer(lambda: each(1, n_col, lambda k: w_col_give(k).wait_send()))


def local(n_row, n_col, features, weight, cotangent, column_of, block_rows, block_cols, edge_blocks):
    rd, width = features.shape
    count, block = edge_blocks.shape[1:3]
    cap = max(2, 2 * rd // n_col)
    slots = n_col * cap
    d_blocks, s_blocks = n_row * rd // block, slots // block
    half = width // PARTS
    piece = width // n_row
    reducers = min(n_col, piece // 8)
    share = piece // reducers
    sizes = (n_row, n_col, cap, block, d_blocks, s_blocks, reducers)
    vmem = pl.BlockSpec(memory_space=pltpu.VMEM)
    hbm = pl.BlockSpec(memory_space=pl.ANY)
    V, D = pltpu.VMEM, pltpu.SemaphoreType.DMA
    return pl.pallas_call(
        functools.partial(kernel, sizes),
        out_shape=(
            jax.ShapeDtypeStruct((rd, width), F32),
            jax.ShapeDtypeStruct((rd, width), F32),
            jax.ShapeDtypeStruct((width, width), F32),
        ),
        in_specs=[hbm, vmem, hbm, vmem, vmem, vmem, hbm],
        out_specs=(vmem, vmem, vmem),
        scratch_shapes=[
            V((rd, width), F32),
            V((rd, width), F32),
            V((count, block, block), F32),
            V((count, block, 2 * block), BF16),
            V((count, block, 2 * block), BF16),
            V((16, 128), I32),
            pltpu.SMEM((16, 128), I32),
            V((slots, rd), BF16),
            V((rd, slots), BF16),
            V((PARTS, slots, half), F32),
            V((PARTS, slots, half), F32),
            V((max(d_blocks, s_blocks), 2 * block, 2 * half), BF16),
            V((count, block, half), F32),
            V((PARTS, n_row, rd, half), F32),
            V((PARTS, 2, rd, half), F32),
            V((PARTS, rd, half), F32),
            V((PARTS, rd, half), F32),
            V((rd, width), F32),
            V((PARTS, n_row, rd, half), F32),
            V((PARTS, slots, half), F32),
            V((PARTS, slots, half), F32),
            V((n_row, piece, width), F32),
            V((n_row, piece, width), F32),
            V((reducers, share, width), F32),
            V((n_col, share, width), F32),
            V((share, width), F32),
            V((n_row, reducers, share, width), F32),
            D((4,)),
            D((PARTS, n_col)), D((PARTS, n_col)),
            D((PARTS, 3)), D((PARTS, 3)),
            D((PARTS, 3)), D((PARTS, 3)),
            D((PARTS, n_col)), D((PARTS, n_col)),
            D((n_row,)), D((n_row,)),
            D((n_col,)), D((n_col,)),
            D((n_col,)), D((n_col,)),
            D((n_row,)), D((n_row,)),
        ],
        compiler_params=pltpu.CompilerParams(
            collective_id=0, has_side_effects=True, vmem_limit_bytes=48 * 2**20
        ),
    )(features, weight, cotangent, column_of, block_rows, block_cols, edge_blocks[0])


def solution(mesh):
    spread = P(("groups", "row", "col"), None)
    placed = (spread, P(), spread, spread, spread, spread, P(("groups", "row", "col"), None, None, None))
    return jax.shard_map(
        functools.partial(local, mesh.shape["row"], mesh.shape["col"]),
        mesh=mesh,
        in_specs=placed,
        out_specs=(spread, spread, P("groups", None)),
        check_vma=False,
    )
```

```python
import functools
import math

import jax
import jax.numpy as jnp
from jax import lax
from jax.experimental import pallas as pl
from jax.experimental.pallas import tpu as pltpu
from jax.sharding import PartitionSpec as P

MESH = pl.DeviceIdType.MESH
F32, BF16, I32 = jnp.float32, jnp.bfloat16, jnp.int32
PARTS = 2
SUBS = 2


def split(value):
    high = value.astype(BF16)
    return high, (value - high.astype(F32)).astype(BF16)


def wide(value):
    return jnp.concatenate(split(value), axis=1)


def mm(a, b, dims=((1,), (0,))):
    return lax.dot_general(a, b, (dims, ((), ())), preferred_element_type=F32)


def mm3(a, b, dims=((1,), (0,))):
    return mm(a[0], b[0], dims) + mm(a[1], b[0], dims) + mm(a[0], b[1], dims)


def each(start, stop, body):
    if stop - start <= 8:
        for i in range(start, stop):
            body(i)
    else:

        def step(i, carry):
            body(i)
            return carry

        lax.fori_loop(start, stop, step, 0)


def partners(n, body):
    if n <= 8:
        for k in sorted(range(1, n), key=lambda k: abs(2 * k - n)):
            body(k)
    else:
        each(1, n, body)


def order_of(own, other, meta, base):
    count = own.shape[1]
    row_at = lax.broadcasted_iota(I32, (count, count), 0)
    lane_at = lax.broadcasted_iota(I32, (count, count), 1)

    def upright(v):
        return jnp.sum(jnp.where(row_at == lane_at, jnp.broadcast_to(v, row_at.shape), 0), axis=1, keepdims=True)

    own_up, other_up = upright(own), upright(other)
    before = (own < own_up) | ((own == own_up) & (lane_at < row_at))
    rank = jnp.sum(before.astype(I32), axis=1, keepdims=True)
    placed = rank == lane_at

    def lay(v):
        return jnp.sum(jnp.where(placed, v, 0), axis=0, keepdims=True)

    meta[base : base + 1, :count] = lay(row_at)
    meta[base + 1 : base + 2, :count] = lay(jnp.broadcast_to(own_up, row_at.shape))
    meta[base + 2 : base + 3, :count] = lay(jnp.broadcast_to(other_up, row_at.shape))
    meta[base + 3 : base + 4, :count] = jnp.maximum(
        jnp.sum((own_up <= lane_at).astype(I32), axis=0, keepdims=True) - 1, 0
    )
    meta[base + 4 : base + 5, :count] = jnp.sum((own_up == lane_at).astype(I32), axis=0, keepdims=True)


def kernel(
    sizes,
    features_hbm, weight_hbm, cotangent_hbm, column_hbm, rows_hbm, cols_hbm, edges_hbm,
    activated_ref, input_ref, wgrad_ref,
    feat, cot, weight_ref, column_ref, rows_ref, cols_ref, edges, edge_f, edge_b, meta, plan, onehot, onehot_t,
    send, recv, table, run, dest, near, mid, far, agg, pre, every, back, back_in,
    wpart, wrow, wsum, wcol, wown, wall,
    load_sem, a_send, a_recv, n_send, n_recv, g_send, g_recv, b_send, b_recv,
    wr_send, wr_recv, wz_send, wz_recv, wy_send, wy_recv, wx_send, wx_recv,
):
    n_row, n_col, cap, block, d_blocks, s_blocks, reducers = sizes
    count = edges.shape[0]
    rd, width = feat.shape
    half = width // PARTS
    row, col = lax.axis_index("row"), lax.axis_index("col")
    p1 = row + 1 - 2 * lax.rem(row, 2)
    p2 = lax.rem(row + 2, n_row)
    p3 = lax.rem(p1 + 2, n_row)

    def remote(src, dst, s_sem, r_sem, where):
        return pltpu.make_async_remote_copy(
            src_ref=src, dst_ref=dst, send_sem=s_sem, recv_sem=r_sem, device_id=where, device_id_type=MESH
        )

    barrier = pltpu.get_barrier_semaphore()
    each(1, n_row, lambda k: pl.semaphore_signal(
        barrier, inc=1, device_id={"row": lax.rem(row + k, n_row)}, device_id_type=MESH))
    each(1, n_col, lambda k: pl.semaphore_signal(
        barrier, inc=1, device_id={"col": lax.rem(col + k, n_col)}, device_id_type=MESH))

    load_f = pltpu.make_async_copy(features_hbm, feat, load_sem.at[0])
    load_e = pltpu.make_async_copy(edges_hbm, edges, load_sem.at[1])
    load_c = pltpu.make_async_copy(cotangent_hbm, cot, load_sem.at[2])
    load_t = pltpu.make_async_copy(column_hbm, column_ref, load_sem.at[4])
    load_r = pltpu.make_async_copy(rows_hbm, rows_ref, load_sem.at[5])
    load_l = pltpu.make_async_copy(cols_hbm, cols_ref, load_sem.at[6])
    load_w = pltpu.make_async_copy(weight_hbm, weight_ref, load_sem.at[7])
    load_t.start()
    load_f.start()
    load_r.start()
    load_l.start()
    load_w.start()
    load_e.start()
    load_c.start()

    same = lax.broadcasted_iota(I32, (rd, rd), 1) == lax.broadcasted_iota(I32, (rd, rd), 0)
    load_t.wait()
    target = jnp.sum(jnp.where(same, jnp.broadcast_to(column_ref[...], (rd, rd)), 0), axis=1, keepdims=True)
    named = lax.broadcasted_iota(I32, (rd, 128), 1) == target
    below = lax.broadcasted_iota(I32, (rd, rd), 1) < lax.broadcasted_iota(I32, (rd, rd), 0)
    earlier = mm(below.astype(F32).astype(BF16), named.astype(F32).astype(BF16))
    rank = jnp.sum(jnp.where(named, earlier, 0.0), axis=1, keepdims=True)
    slot = target * cap + rank.astype(I32)
    slot_row = jnp.sum(jnp.where(same, jnp.broadcast_to(slot, (rd, rd)), 0), axis=0, keepdims=True)
    slots = n_col * cap
    onehot[...] = (lax.broadcasted_iota(I32, (slots, rd), 0) == slot_row).astype(F32).astype(BF16)
    load_f.wait()

    def route_copy(part, k):
        to = lax.rem(col + k, n_col)
        return remote(
            send.at[part, pl.ds(pl.multiple_of(to * cap, cap), cap)],
            recv.at[part, pl.ds(pl.multiple_of(col * cap, cap), cap)],
            a_send.at[part, to], a_recv.at[part, col], {"col": to},
        )

    def route_arrival(part, k):
        of = lax.rem(col + k, n_col)
        return remote(
            send.at[part, pl.ds(pl.multiple_of(of * cap, cap), cap)],
            recv.at[part, pl.ds(pl.multiple_of(of * cap, cap), cap)],
            a_send.at[part, of], a_recv.at[part, of], {"col": of},
        )

    mine = pl.ds(pl.multiple_of(col * cap, cap), cap)
    for part in range(PARTS):
        both = mm(onehot[...], wide(feat[:, part * half : (part + 1) * half]))
        send[part] = both[:, :half] + both[:, half:]
        if part == 0:
            pl.semaphore_wait(barrier, n_row + n_col - 2)
        partners(n_col, lambda k: route_copy(part, k).start())
        recv[part, mine] = send[part, mine]

    load_r.wait()
    load_l.wait()
    order_of(rows_ref[...], cols_ref[...], meta, 0)
    order_of(cols_ref[...], rows_ref[...], meta, 8)
    load_m = pltpu.make_async_copy(meta, plan, load_sem.at[3])
    load_m.start()
    onehot_t[...] = (lax.broadcasted_iota(I32, (rd, slots), 1) == slot).astype(F32).astype(BF16)
    load_e.wait()

    def prepare(k, carry):
        value = edges[k]
        edge_f[k] = wide(value)
        edge_b[k] = wide(value.T)
        return carry

    lax.fori_loop(0, count, prepare, 0)
    load_m.wait()
    load_c.wait()
    load_w.wait()
    w_pair = split(weight_ref[...])

    def fill(at, value):
        pair = wide(value)
        table[at, :block] = pair
        table[at, block:] = pair

    def multiply(edge_ref, base):
        def step(p, total):
            product = mm(edge_ref[plan[base, p]], table[plan[base + 2, p]])
            kept = plan[base + 1, p] == plan[base + 1, jnp.maximum(p - 1, 0)]
            total = jnp.where(kept, total, 0.0) + product[:, :half] + product[:, half:]
            run[p] = total
            return total

        lax.fori_loop(0, count, step, jnp.zeros((block, half), F32), unroll=8)

    def taken(base, at):
        return jnp.where(plan[base + 4, at] > 0, run[plan[base + 3, at]], 0.0)

    per = rd // block

    sub = rd // SUBS
    per_sub = per // SUBS

    def near_copy(part, which, at):
        rows = slice(at * sub, (at + 1) * sub)
        return remote(
            dest.at[part, p3 if which == 0 else p1, rows], near.at[part, which, rows],
            n_send.at[part, which, at], n_recv.at[part, which, at], {"row": p1},
        )

    def far_copy(part, at):
        rows = slice(at * sub, (at + 1) * sub)
        return remote(
            mid.at[part, rows], far.at[part, rows], n_send.at[part, 2, at], n_recv.at[part, 2, at], {"row": p2}
        )

    for part in range(PARTS):
        partners(n_col, lambda k: route_arrival(part, k).wait_recv())
        for s in range(s_blocks):
            fill(s, recv[part, s * block : (s + 1) * block])
        multiply(edge_f, 0)
        for which, owner in enumerate((p3, p2, p1, row)):
            for at in range(SUBS):
                for i in range(at * per_sub, (at + 1) * per_sub):
                    dest[part, owner, i * block : (i + 1) * block] = taken(0, owner * per + i)
                if which == 0:
                    near_copy(part, 0, at).start()
                if which == 2:
                    near_copy(part, 1, at).start()
            if which == 1:
                for at in range(SUBS):
                    rows = slice(at * sub, (at + 1) * sub)
                    near_copy(part, 0, at).wait_recv()
                    mid[part, rows] = dest[part, p2, rows] + near[part, 0, rows]
                    far_copy(part, at).start()

    def give(part, which, at):
        owner, rows = row if which < 2 else p2, slice(at * sub, (at + 1) * sub)
        return remote(
            every.at[part, owner, rows], every.at[part, owner, rows],
            g_send.at[part, which, at], g_recv.at[part, which, at], {"row": p2 if which == 0 else p1},
        )

    def take(part, which, at):
        owner, rows = (p2, p1, p3)[which], slice(at * sub, (at + 1) * sub)
        return remote(
            every.at[part, owner, rows], every.at[part, owner, rows],
            g_send.at[part, which, at], g_recv.at[part, which, at], {"row": p2 if which == 0 else p1},
        )

    scale = math.sqrt(2.0 / math.pi)
    for at in range(SUBS):
        rows = slice(at * sub, (at + 1) * sub)
        for part in range(PARTS):
            near_copy(part, 1, at).wait_recv()
            far_copy(part, at).wait_recv()
            agg[rows, part * half : (part + 1) * half] = (
                dest[part, row, rows] + near[part, 1, rows] + far[part, rows]
            )
        x = mm3(split(agg[rows]), w_pair)
        square = x * x
        t = jnp.tanh(scale * (x + 0.044715 * (square * x)))
        activated_ref[rows] = 0.5 * x * (1.0 + t)
        slope = 0.5 * (1.0 + t) + 0.5 * x * (1.0 - t * t) * (scale * (1.0 + 3.0 * 0.044715 * square))
        pre[rows] = cot[rows] * slope
        grad = mm3(split(pre[rows]), w_pair, ((1,), (1,)))
        for part in range(PARTS):
            every[part, row, rows] = grad[:, part * half : (part + 1) * half]
        give(0, 0, at).start()
        give(0, 1, at).start()
    for part in range(1, PARTS):
        for at in range(SUBS):
            give(part, 0, at).start()
            give(part, 1, at).start()

    def back_copy(part, k):
        to = lax.rem(col + k, n_col)
        return remote(
            back.at[part, pl.ds(pl.multiple_of(to * cap, cap), cap)],
            back_in.at[part, pl.ds(pl.multiple_of(col * cap, cap), cap)],
            b_send.at[part, to], b_recv.at[part, col], {"col": to},
        )

    def back_arrival(part, k):
        of = lax.rem(col + k, n_col)
        return remote(
            back.at[part, pl.ds(pl.multiple_of(of * cap, cap), cap)],
            back_in.at[part, pl.ds(pl.multiple_of(of * cap, cap), cap)],
            b_send.at[part, of], b_recv.at[part, of], {"col": of},
        )

    piece = width // reducers
    share = piece // n_row

    def w_col_copy(to):
        return remote(wpart.at[to], wcol.at[col], wz_send.at[to], wz_recv.at[col], {"col": to})

    def w_col_arrival(of):
        return remote(wpart.at[0], wcol.at[of], wz_send.at[0], wz_recv.at[of], {"col": of})

    def w_row_copy(k):
        to = lax.rem(row + k, n_row)
        return remote(wsum.at[to], wrow.at[row], wr_send.at[to], wr_recv.at[row], {"row": to})

    def w_row_arrival(k):
        of = lax.rem(row + k, n_row)
        return remote(wsum.at[of], wrow.at[of], wr_send.at[of], wr_recv.at[of], {"row": of})

    def w_col_give(k):
        to = lax.rem(col + k, n_col)
        return remote(wown, wall.at[row, col], wy_send.at[to], wy_recv.at[col], {"col": to})

    def w_col_take(of):
        return remote(wown, wall.at[row, of], wy_send.at[of], wy_recv.at[of], {"col": of})

    def w_row_give(k):
        to = lax.rem(row + k, n_row)
        return remote(wall.at[row], wall.at[row], wx_send.at[to], wx_recv.at[row], {"row": to})

    def w_row_take(k):
        of = lax.rem(row + k, n_row)
        return remote(wall.at[of], wall.at[of], wx_send.at[of], wx_recv.at[of], {"row": of})

    def reducer(body):
        if reducers == n_col:
            body()
        else:
            pl.when(col < reducers)(body)

    def others(body):
        if reducers == n_col:
            partners(n_col, lambda k: body(lax.rem(col + k, n_col)))
        else:
            each(0, reducers, lambda j: pl.when(col != j)(lambda: body(j)))

    def w_first():
        wlocal = mm3(split(agg[...]), split(pre[...]), ((0,), (0,)))
        for j in range(reducers):
            wpart[j] = wlocal[j * piece : (j + 1) * piece]
        others(lambda j: w_col_copy(j).start())

    def w_second():
        partners(n_col, lambda k: w_col_arrival(lax.rem(col + k, n_col)).wait_recv())
        wcol[col] = wpart[col]
        total = wcol[0]
        for j in range(1, n_col):
            total = total + wcol[j]
        for r in range(n_row):
            wsum[r] = total[r * share : (r + 1) * share]
        each(1, n_row, lambda k: w_row_copy(k).start())

    def w_third():
        each(1, n_row, lambda k: w_row_arrival(k).wait_recv())
        wrow[row] = wsum[row]
        total = wrow[0]
        for r in range(1, n_row):
            total = total + wrow[r]
        wown[...] = total * (float(rd * n_row * n_col) ** -0.5)
        each(1, n_col, lambda k: w_col_give(k).start())
        wall[row, col] = wown[...]

    def w_fourth():
        others(lambda j: w_col_take(j).wait_recv())
        each(1, n_row, lambda k: w_row_give(k).start())

    w_first()
    for part in range(PARTS):
        for at in range(SUBS):
            take(part, 0, at).wait_recv()
            give(part, 2, at).start()
        if part == 1:
            reducer(w_third)
        for which, owner in ((3, row), (1, p1), (0, p2), (2, p3)):
            for at in range(SUBS):
                if which in (1, 2):
                    take(part, which, at).wait_recv()
                for i in range(at * per_sub, (at + 1) * per_sub):
                    fill(owner * per + i, every[part, owner, i * block : (i + 1) * block])
        multiply(edge_b, 8)
        for s in range(s_blocks):
            back[part, s * block : (s + 1) * block] = taken(8, s)
        partners(n_col, lambda k: back_copy(part, k).start())
        back_in[part, mine] = back[part, mine]
        if part == 0:
            reducer(w_second)

    for part in range(PARTS):
        partners(n_col, lambda k: back_arrival(part, k).wait_recv())
        both = mm(onehot_t[...], wide(back_in[part]))
        input_ref[:, part * half : (part + 1) * half] = both[:, :half] + both[:, half:]
        if part == 0:
            w_fourth()
    each(1, n_row, lambda k: w_row_take(k).wait_recv())
    for r in range(n_row):
        for j in range(reducers):
            wgrad_ref[j * piece + r * share : j * piece + (r + 1) * share] = wall[r, j]

    for part in range(PARTS):
        partners(n_col, lambda k: route_copy(part, k).wait_send())
        partners(n_col, lambda k: back_copy(part, k).wait_send())
        for at in range(SUBS):
            near_copy(part, 0, at).wait_send()
            near_copy(part, 1, at).wait_send()
            far_copy(part, at).wait_send()
            for which in range(3):
                give(part, which, at).wait_send()
    others(lambda j: w_col_copy(j).wait_send())

    def last():
        each(1, n_row, lambda k: w_row_copy(k).wait_send())
        each(1, n_col, lambda k: w_col_give(k).wait_send())

    reducer(last)
    each(1, n_row, lambda k: w_row_give(k).wait_send())


def local(n_row, n_col, features, weight, cotangent, column_of, block_rows, block_cols, edge_blocks):
    rd, width = features.shape
    count, block = edge_blocks.shape[1:3]
    cap = max(2, 2 * rd // n_col)
    slots = n_col * cap
    d_blocks, s_blocks = n_row * rd // block, slots // block
    half = width // PARTS
    reducers = min(n_col, width // (8 * n_row))
    piece = width // reducers
    share = piece // n_row
    sizes = (n_row, n_col, cap, block, d_blocks, s_blocks, reducers)
    vmem = pl.BlockSpec(memory_space=pltpu.VMEM)
    hbm = pl.BlockSpec(memory_space=pltpu.HBM)
    V, D = pltpu.VMEM, pltpu.SemaphoreType.DMA
    return pl.pallas_call(
        functools.partial(kernel, sizes),
        out_shape=(
            jax.ShapeDtypeStruct((rd, width), F32),
            jax.ShapeDtypeStruct((rd, width), F32),
            jax.ShapeDtypeStruct((width, width), F32),
        ),
        in_specs=[hbm] * 7,
        out_specs=(vmem, vmem, vmem),
        scratch_shapes=[
            V((rd, width), F32),
            V((rd, width), F32),
            V((width, width), F32),
            V((1, rd), I32),
            V((1, count), I32),
            V((1, count), I32),
            V((count, block, block), F32),
            V((count, block, 2 * block), BF16),
            V((count, block, 2 * block), BF16),
            V((16, 128), I32),
            pltpu.SMEM((16, 128), I32),
            V((slots, rd), BF16),
            V((rd, slots), BF16),
            V((PARTS, slots, half), F32),
            V((PARTS, slots, half), F32),
            V((max(d_blocks, s_blocks), 2 * block, 2 * half), BF16),
            V((count, block, half), F32),
            V((PARTS, n_row, rd, half), F32),
            V((PARTS, 2, rd, half), F32),
            V((PARTS, rd, half), F32),
            V((PARTS, rd, half), F32),
            V((rd, width), F32),
            V((rd, width), F32),
            V((PARTS, n_row, rd, half), F32),
            V((PARTS, slots, half), F32),
            V((PARTS, slots, half), F32),
            V((reducers, piece, width), F32),
            V((n_row, share, width), F32),
            V((n_row, share, width), F32),
            V((n_col, piece, width), F32),
            V((share, width), F32),
            V((n_row, reducers, share, width), F32),
            D((8,)),
            D((PARTS, n_col)), D((PARTS, n_col)),
            D((PARTS, 3, SUBS)), D((PARTS, 3, SUBS)),
            D((PARTS, 3, SUBS)), D((PARTS, 3, SUBS)),
            D((PARTS, n_col)), D((PARTS, n_col)),
            D((n_row,)), D((n_row,)),
            D((n_col,)), D((n_col,)),
            D((n_col,)), D((n_col,)),
            D((n_row,)), D((n_row,)),
        ],
        compiler_params=pltpu.CompilerParams(
            collective_id=0, has_side_effects=True, vmem_limit_bytes=60 * 2**20
        ),
    )(features, weight, cotangent, column_of.reshape(1, rd), block_rows, block_cols, edge_blocks[0])


def solution(mesh):
    spread = P(("groups", "row", "col"), None)
    placed = (spread, P(), spread, spread, spread, spread, P(("groups", "row", "col"), None, None, None))
    return jax.shard_map(
        functools.partial(local, mesh.shape["row"], mesh.shape["col"]),
        mesh=mesh,
        in_specs=placed,
        out_specs=(spread, spread, P("groups", None)),
        check_vma=False,
    )
```
